128 devices in a mesh: expert: 16 (over y, z), etensor: 8 (over x, core).
Axes of the slice: x: 4, y: 4, z: 4, core: 2. Of those that a mesh axis runs over, the one named last changes fastest.
Arguments:
- tokens: bfloat16 [2048, 7168], P('expert', 'etensor'), may hold values from -6 to 6
- expert_ids: int32 [2048, 8], P('expert'), may hold values from 0 to 31, all different within a row; in each aligned block of 128 rows (0 to 127, 128 to 255, ...) at most 36 rows name the same one
- gate_weights: float32 [2048, 8], P('expert'), may hold values from 0.1 to 1
- gate_up: bfloat16 [32, 7168, 2, 2048], P('expert', None, None, 'etensor'), may hold values from -0.0625 to 0.0625
- down_proj: bfloat16 [32, 2048, 7168], P('expert', 'etensor'), may hold values from -0.125 to 0.125
Outputs:
- mixed: bfloat16 [2048, 7168], P('expert', 'etensor')
The draws below stay inside these ranges and needn't reach their ends.
Inputs may be any that keep to these rules, and one draw needn't show every extreme that they name: `expert_ids`: each row names 8 different experts. Within each aligned block of 128 rows no expert is named by more than 36 rows, and in some block some expert is named by exactly 36 rows.
All inputs are finite; a program needn't handle non-finite values.
Results may differ from the reference program's by a relative error of at most 0.019.
Values may be sent and summed in bfloat16 or wider, within the bound.
A program may use at most 320 MiB of HBM per device.

```python
import math
import jax
import jax.numpy as jnp
import numpy as np
from jax import lax

D = 7168
FF = 2048
TOP = 8
TOK_DEV = 128
EXPERTS = 32
CAP = 36
TOKENS = 2048
N_EXPERT = 16
N_ETENSOR = 8


def block_levels(rng, extent, shards, smallest, high):
    def one(axis_at, parts):
        draws = jax.random.uniform(jax.random.fold_in(jax.random.fold_in(rng, 6), axis_at), (parts,), jnp.float32, smallest / len(shards), high / len(shards))
        return jnp.repeat(jnp.exp(draws), extent[axis_at] // parts).reshape((-1,) + (1,) * (len(extent) - axis_at - 1))

    level = one(*shards[0])
    for cut in shards[1:]:
        level = level * one(*cut)
    return level


def shared_out(own_key, own, number, rows, count, top, limit, lean):
    ranking = jax.random.permutation(own_key, count)
    packed, ordinary = shares(count, rows * top, limit, lean, True), shares(count, rows * top, limit, lean, False)
    places = jnp.arange(count)

    def named(sizes, rotation):
        used = int((sizes > 0).sum())
        fixed = max(1, used // 4)
        passed = fixed + (places - fixed + rotation * (used - fixed)) % max(1, count - fixed)
        return jnp.zeros((count,), jnp.int32).at[ranking[jnp.where(places < fixed, places, passed)]].set(jnp.asarray(sizes, jnp.int32))

    sizes = jnp.where(number % 4 == 0, named(packed, number // 4), named(ordinary, number - number // 4 - 1))
    mixed = jax.random.permutation(jax.random.fold_in(own, 3), count)
    giver, receiver = mixed[0:count // 2 * 2:2], mixed[1:count // 2 * 2:2]
    margin = jnp.minimum(sizes[giver] - 1, limit - sizes[receiver]) // 2
    margin = jnp.where((giver == ranking[0]) | (receiver == ranking[0]) | (sizes[receiver] == 0), 0, jnp.maximum(margin, 0))
    passed = jax.random.randint(jax.random.fold_in(own, 4), (count // 2,), 0, 1 << 20) % (margin + 1)
    sizes = sizes.at[giver].add(-passed).at[receiver].add(passed)
    labels = jnp.searchsorted(jnp.cumsum(sizes), jnp.arange(rows * top), side="right").astype(jnp.int32)
    grid = labels.reshape(top, rows).T
    grid = grid[jax.random.permutation(jax.random.fold_in(own, 1), rows)]
    rotation = jax.random.randint(jax.random.fold_in(own, 2), (rows, 1), 0, top)
    return jnp.take_along_axis(grid, (jnp.arange(top)[None, :] + rotation) % top, axis=1)


def shares(number_of, total, reach, skew, full):
    portions = [(1 << 20) // math.isqrt(grade ** skew) + 1 for grade in range(1, number_of + 1)]
    largest = reach if full else min(reach, max(-(-total // number_of), total * portions[0] // sum(portions)))
    least = 1 if total - largest >= number_of - 1 else 0
    counts, surplus = [largest] + [least] * (number_of - 1), total - largest - least * (number_of - 1)
    while surplus > 0:
        free = [i for i in range(1, number_of) if counts[i] < largest] or [i for i in range(1, number_of) if counts[i] < reach]
        mass, remaining = sum([portions[i] for i in free]), surplus
        for i in free:
            extra = min(reach - counts[i], max(1, remaining * portions[i] // mass), surplus)
            counts[i] = counts[i] + extra
            surplus = surplus - extra
    return np.array(counts)


def centred(key, dims, scale, bound, split=(), kind=jnp.bfloat16):
    gain = block_levels(key, dims, split, -0.22, 0.18) if split else 1.0
    entries = jax.random.normal(key, dims, jnp.float32) * scale * gain
    return jnp.minimum(jnp.maximum(entries, -bound), bound).astype(kind)


def setup_inputs(seed: int = 0) -> dict:
    streams_of = jax.random.split(jax.random.key(seed), 6)
    tokens = centred(streams_of[0], (TOKENS, D), 1.0, 6.0, ((0, 16), (1, 8)))
    expert_ids_keys = jax.random.split(jax.random.fold_in(streams_of[1], 1), TOKENS // TOK_DEV)
    expert_ids_turns = jax.random.permutation(jax.random.fold_in(streams_of[1], 3), TOKENS // TOK_DEV)
    expert_ids = jax.vmap(lambda own, number: shared_out(jax.random.fold_in(streams_of[1], 2), own, number, TOK_DEV, EXPERTS, TOP, CAP, 2))(expert_ids_keys, expert_ids_turns).reshape((TOKENS, TOP))
    gate_weights = jnp.clip(jnp.exp(math.log(1.0) - 2.3025851 * jax.random.uniform(streams_of[2], (TOKENS, TOP), jnp.float32) ** block_levels(streams_of[2], (TOKENS, TOP), ((0, 16),), -0.2, 0.2)), 0.1, 1.0)
    gate_up = centred(streams_of[3], (EXPERTS, D, 2, FF), D ** -0.5, 0.0625, ((0, 16), (3, 8)))
    down_proj = centred(streams_of[4], (EXPERTS, FF, D), FF ** -0.5, 0.125, ((0, 16), (1, 8)))
    return dict(tokens=tokens, expert_ids=expert_ids, gate_weights=gate_weights, gate_up=gate_up, down_proj=down_proj)


def expert_ffn(row_block, gate_up_one, down_one):
    n_rows = row_block.shape[0]
    projected = jnp.dot(row_block.astype(jnp.float32), gate_up_one.reshape(D, 2 * FF).astype(jnp.float32)).reshape(n_rows, 2, FF)
    hidden = (jax.nn.silu(projected[:, 0]) * projected[:, 1]).astype(jnp.bfloat16)
    hidden_f = hidden.astype(jnp.float32).reshape(n_rows, N_ETENSOR, FF // N_ETENSOR)
    down_f = down_one.astype(jnp.float32).reshape(N_ETENSOR, FF // N_ETENSOR, D)
    shard_parts = jnp.einsum("rsf,sfd->srd", hidden_f, down_f)
    rounded = lax.optimization_barrier(shard_parts.astype(jnp.bfloat16))
    return jnp.sum(rounded.astype(jnp.float32), axis=0)


def reference(tokens, expert_ids, gate_weights, gate_up, down_proj):
    flat_ids = expert_ids.reshape(-1)
    flat_gates = gate_weights.reshape(-1)
    most_rows = CAP * N_EXPERT

    def per_expert(mixed_sum, inputs):
        expert_idx, gate_up_one, down_one = inputs
        matched = flat_ids == expert_idx
        picked = jnp.nonzero(matched, size=most_rows, fill_value=0)[0].astype(jnp.int32)
        n_picked = jnp.sum(matched.astype(jnp.int32))
        is_live = jnp.arange(most_rows, dtype=jnp.int32) < n_picked
        token_idx = (picked // TOP).astype(jnp.int32)
        expert_rows = expert_ffn(tokens[token_idx], gate_up_one, down_one)
        weight = jnp.where(is_live, flat_gates[picked], jnp.zeros_like(flat_gates[picked]))
        mixed_sum = mixed_sum.at[token_idx].add(weight[:, None] * expert_rows)
        return mixed_sum, None

    start_sum = jnp.zeros((TOKENS, D), jnp.float32)
    experts_iota = jnp.arange(EXPERTS, dtype=jnp.int32)
    mixed_sum, _ = lax.scan(per_expert, start_sum, (experts_iota, gate_up, down_proj))
    return mixed_sum.astype(jnp.bfloat16)
```

```python
import jax
import jax.numpy as jnp
from jax import lax
from jax.sharding import PartitionSpec as P


def on_device(tokens, expert_ids, gate_weights, gate_up, down_proj):
    n_owner = lax.axis_size("expert")
    n_shard = lax.axis_size("etensor")
    tok_dev, width = tokens.shape
    top_k = expert_ids.shape[1]
    exp_dev = gate_up.shape[0]
    experts = exp_dev * n_owner
    capacity = 9 * tok_dev * top_k // (8 * experts)
    all_slots = experts * capacity
    per_owner = exp_dev * capacity
    hits = expert_ids[:, :, None] == jnp.arange(experts, dtype=jnp.int32)
    named = jnp.sum(hits.astype(jnp.float32), axis=1)
    gates = jnp.sum(jnp.where(hits, gate_weights[:, :, None], 0.0), axis=1)
    rows = jnp.arange(tok_dev)
    before = (rows[None, :] < rows[:, None]).astype(jnp.float32)
    position = jnp.dot(before, named, preferred_element_type=jnp.float32)
    at_slot = (position[:, :, None] == jnp.arange(capacity, dtype=jnp.float32)) & (named[:, :, None] > 0)
    placing = at_slot.astype(jnp.bfloat16).reshape(tok_dev, all_slots)
    gate_hi = gates.astype(jnp.bfloat16)
    gate_lo = (gates - gate_hi.astype(jnp.float32)).astype(jnp.bfloat16)
    zero = jnp.zeros((), jnp.bfloat16)
    taking_hi = jnp.where(at_slot, gate_hi[:, :, None], zero).reshape(tok_dev, all_slots)
    taking_lo = jnp.where(at_slot, gate_lo[:, :, None], zero).reshape(tok_dev, all_slots)

    placed = jnp.einsum("ts,td->sd", placing, tokens, preferred_element_type=jnp.float32)
    arrived = lax.all_to_all(
        placed.astype(jnp.bfloat16).reshape(n_owner, per_owner, width),
        "expert",
        split_axis=0,
        concat_axis=0,
        tiled=True,
    )
    full = lax.all_gather(arrived, "etensor", axis=0, tiled=False)
    full = full.reshape(n_shard, n_owner, exp_dev, capacity, width)
    split_up = gate_up.reshape(exp_dev, n_shard, width, 2, gate_up.shape[3])
    projected = jnp.einsum(
        "sojcd,jsdgf->ojcgf", full, split_up, preferred_element_type=jnp.float32
    )
    hidden = (jax.nn.silu(projected[:, :, :, 0, :]) * projected[:, :, :, 1, :]).astype(jnp.bfloat16)
    split_down = down_proj.reshape(exp_dev, down_proj.shape[1], n_shard, width)
    partial_value = jnp.einsum(
        "ojcf,jfsd->sojcd", hidden, split_down, preferred_element_type=jnp.float32
    ).astype(jnp.bfloat16)
    summed = lax.psum_scatter(
        partial_value.reshape(n_shard, n_owner, per_owner, width),
        "etensor",
        scatter_dimension=0,
        tiled=False,
    )
    returned = lax.all_to_all(summed, "expert", split_axis=0, concat_axis=0, tiled=True)
    returned = returned.reshape(all_slots, width)
    mixed = jnp.dot(taking_hi, returned, preferred_element_type=jnp.float32)
    mixed = mixed + jnp.dot(taking_lo, returned, preferred_element_type=jnp.float32)
    return mixed.astype(jnp.bfloat16)


def solution(mesh):
    placed = (
        P("expert", "etensor"),
        P("expert", None),
        P("expert", None),
        P("expert", None, None, "etensor"),
        P("expert", "etensor", None),
    )
    return jax.shard_map(
        on_device, mesh=mesh, in_specs=placed, out_specs=P("expert", "etensor"), check_vma=False
    )
```

```python
import jax
import jax.numpy as jnp
from jax import lax
from jax.experimental import pallas as pl
from jax.experimental.pallas import tpu as pltpu
from jax.sharding import PartitionSpec as P

MESH = pl.DeviceIdType.MESH
F32, BF16 = jnp.float32, jnp.bfloat16
N = 4
SUB = 48


def dot(a, b):
    return jnp.dot(a, b, preferred_element_type=F32)


def kernel(cap, tokens, route, gate_up, down, out, X, SB, OP, IN, RET, PL, T, RT, ZR, CB, ACC, HID, SLOT, GATE,
           WG, WD, wsem, ssem, rsem):
    half = N * cap
    rows = 2 * half
    top = route.shape[0] // 2
    tok, width = tokens.shape
    ff = down.shape[1]
    e, s = lax.axis_index("expert"), lax.axis_index("etensor")
    y, z, x, c = e // N, e % N, s // 2, s % 2

    def at_x(p, other):
        chip = (x + (0, N - 1, 1, 2)[p]) % N
        return chip * 2 + (1 - c if other else c)

    own, left, right, sibling = (e, s), (e, at_x(1, False)), (e, at_x(2, False)), (e, at_x(0, True))
    z_up = [(y * N + (z + d) % N, s) for d in range(N)]
    z_down = [(y * N + (z + N - d) % N, s) for d in range(N)]
    y_up = [((y + d) % N * N + z, s) for d in range(N)]
    y_down = [((y + N - d) % N * N + z, s) for d in range(N)]

    loads = []
    for q in range(2 * N):
        col = pl.multiple_of(at_x(q % N, q >= N) * width, 128)
        loads.append(pltpu.make_async_copy(gate_up.at[:, pl.ds(col, width), :], WG.at[q], wsem.at[2 * q]))
        loads.append(pltpu.make_async_copy(down.at[:, :, pl.ds(col, width)], WD.at[q], wsem.at[2 * q + 1]))
    for load in loads:
        load.start()

    barrier = pltpu.get_barrier_semaphore()
    friends = z_up[1:] + y_up[1:] + [left, right, sibling]
    for f in friends:
        pl.semaphore_signal(barrier, inc=1, device_id=f, device_id_type=MESH)
    pl.semaphore_wait(barrier, len(friends))

    copies = {}

    def plan(key, src, dst, device):
        i = len(copies)
        copies[key] = pltpu.make_async_remote_copy(
            src_ref=src, dst_ref=dst, send_sem=ssem.at[i], recv_sem=rsem.at[i], device_id=device, device_id_type=MESH
        )

    lo, hi = pl.ds(0, half), pl.ds(half, half)
    for d in range(1, N):
        plan(("zt", d), tokens, T.at[d], z_up[d])
        plan(("zr", d), route, RT.at[d], z_up[d])
        plan(("zo", d), T.at[d], ZR.at[d - 1], z_down[d])
        plan(("yt", d), PL.at[d - 1], X.at[0, d], y_up[d])
        plan(("yo", d), X.at[0, d], RET.at[d], y_down[d])
    for g in range(N):
        plan(("r", g), X.at[0, g], X.at[1, g], right)
        plan(("l", g), X.at[0, g], X.at[2, g], left)
        plan(("rr", g), X.at[1, g, lo], X.at[3, g, lo], right)
        plan(("ll", g), X.at[2, g, hi], X.at[3, g, hi], left)
        for p in range(N):
            plan(("s", g, p), X.at[p, g], X.at[N + p, g], sibling)
        plan(("S", g), X.at[pl.ds(N, N), g], SB.at[:, g], sibling)
        plan(("or", g), X.at[3, g, lo], OP.at[0, g], right)
        plan(("ol", g), X.at[3, g, hi], OP.at[1, g], left)
        plan(("ir", g, 0), X.at[2, g, hi], IN.at[0, g, hi], right)
        plan(("il", g, 0), X.at[1, g, lo], IN.at[1, g, lo], left)
        plan(("ir", g, 1), X.at[2, g, lo], IN.at[0, g, lo], right)
        plan(("il", g, 1), X.at[1, g, hi], IN.at[1, g, hi], left)

    def start(*key):
        copies[key].start()

    def sent(*key):
        copies[key].wait_send()

    def got(*key):
        copies[key].wait_recv()

    for d in (1, 3, 2):
        start("zr", d)
        start("zt", d)

    T[0] = tokens[...]
    RT[0] = route[...]

    line = lax.broadcasted_iota(jnp.int32, (2 * N, tok), 0)
    expert = (2 * (N * ((y + line // 2) % N) + z) + line % 2).astype(F32)
    before = lax.broadcasted_iota(jnp.int32, (tok, tok), 0) < lax.broadcasted_iota(jnp.int32, (tok, tok), 1)
    before = jnp.where(before, 1.0, 0.0).astype(BF16)
    for d in range(N):
        if d:
            got("zr", d)
        named = jnp.zeros((2 * N, tok), F32)
        gate = jnp.zeros((2 * N, tok), F32)
        for k in range(top):
            hit = RT[d, k : k + 1, :] == expert
            named = named + jnp.where(hit, 1.0, 0.0)
            gate = gate + jnp.where(hit, RT[d, top + k : top + k + 1, :], 0.0)
        position = dot(named.astype(BF16), before)
        SLOT[:, d * tok : (d + 1) * tok] = jnp.where(named > 0.0, position + float(d * cap), -1.0)
        GATE[:, d * tok : (d + 1) * tok] = gate

    slot_of = lax.broadcasted_iota(jnp.int32, (half, N * tok), 0).astype(F32)

    def place(g, to):
        for j in range(2):
            i = 2 * g + j
            takes = jnp.where(slot_of == SLOT[i : i + 1, :], 1.0, 0.0).astype(BF16)
            to[j * half : (j + 1) * half, :] = dot(takes, T[...].reshape(N * tok, width)).astype(BF16)

    for d in range(1, N):
        got("zt", d)

    place(0, X.at[0, 0])

    def stage_a(g):
        if g:
            got("yt", g)
        start("r", g)
        start("l", g)
        start("s", g, 0)

    stage_a(0)
    for g in (1, 3, 2):
        place(g, PL.at[g - 1])
        start("yt", g)

    def stage_b(g):
        got("r", g)
        start("rr", g)
        got("l", g)
        start("ll", g)
        start("s", g, 1)
        start("s", g, 2)

    def stage_c(g):
        got("rr", g)
        got("ll", g)
        start("s", g, 3)

    def stage_d(g):
        for p in range(N):
            got("s", g, p)
        ACC[...] = jnp.zeros_like(ACC)

        @pl.loop(0, 2 * N)
        def _(q):
            for j in range(2):
                piece = pl.ds(j * half, half)
                ACC[piece, :] += dot(X[q, g, piece, :], WG[q, j])

        a = ACC[...]
        HID[...] = (jax.nn.silu(a[:, :ff]) * a[:, ff:]).astype(BF16)

        def down_of(q):
            for j in range(2):
                piece = pl.ds(j * half, half)
                X[q, g, piece, :] = dot(HID[piece, :], WD[q, j]).astype(BF16)

        pl.loop(N, 2 * N)(down_of)
        start("S", g)
        for k in ("r", "l", "rr", "ll"):
            sent(k, g)
        for p in range(N):
            sent("s", g, p)
        pl.loop(0, N)(down_of)

    def add(n, to, terms):
        @pl.loop(0, n // SUB)
        def _(i):
            at = pl.ds(pl.multiple_of(i * SUB, SUB), SUB)
            total = terms[0][at, :].astype(F32)
            for t in terms[1:]:
                total = total + t[at, :].astype(F32)
            to[at, :] = total.astype(BF16)

    def stage_e(g):
        got("S", g)
        add(rows, X.at[3, g], [X.at[3, g], SB.at[3, g]])
        start("or", g)
        start("ol", g)
        add(half, X.at[2, g, hi], [X.at[2, g, hi], SB.at[2, g, hi]])
        start("ir", g, 0)
        add(half, X.at[1, g, lo], [X.at[1, g, lo], SB.at[1, g, lo]])
        start("il", g, 0)

    def stage_f(g):
        got("or", g)
        add(half, X.at[2, g, lo], [X.at[2, g, lo], SB.at[2, g, lo], OP.at[0, g]])
        start("ir", g, 1)
        got("ol", g)
        add(half, X.at[1, g, hi], [X.at[1, g, hi], SB.at[1, g, hi], OP.at[1, g]])
        start("il", g, 1)

    def stage_g(g):
        for k in range(2):
            got("ir", g, k)
            got("il", g, k)
        add(rows, X.at[0, g] if g else RET.at[0], [X.at[0, g], SB.at[0, g], IN.at[0, g], IN.at[1, g]])
        if g:
            start("yo", g)

    def stage_h(g):
        if g:
            got("yo", g)
        for j in range(2):
            i = 2 * g + j
            takes = jnp.where(slot_of == SLOT[i : i + 1, :], GATE[i : i + 1, :], 0.0).astype(BF16)
            product = lax.dot_general(
                takes, RET[g, j * half : (j + 1) * half, :], (((0,), (0,)), ((), ())), preferred_element_type=F32
            )
            CB[...] = product if i == 0 else CB[...] + product

    stage_a(1)
    stage_b(0)
    stage_a(2)
    stage_b(1)
    for d in loads:
        d.wait()
    stage_c(0)
    stage_d(0)
    stage_a(3)
    stage_b(2)
    stage_e(0)
    stage_c(1)
    stage_d(1)
    stage_f(0)
    stage_b(3)
    stage_e(1)
    stage_c(2)
    stage_d(2)
    stage_g(0)
    stage_f(1)
    stage_e(2)
    stage_c(3)
    stage_d(3)
    stage_g(1)
    stage_f(2)
    stage_e(3)
    stage_h(0)
    stage_h(1)
    stage_g(2)
    stage_f(3)
    stage_h(2)
    stage_g(3)
    stage_h(3)
    for d in range(1, N):
        sent("zt", d)
        T[d] = CB[d * tok : (d + 1) * tok, :].astype(BF16)
        start("zo", d)
    total = CB[0:tok, :]
    for d in range(1, N):
        got("zo", d)
        total = total + ZR[d - 1].astype(F32)
    out[...] = total.astype(BF16)

    for d in range(1, N):
        for k in ("zr", "zo", "yt", "yo"):
            sent(k, d)
    for g in range(N):
        sent("S", g)
        sent("or", g)
        sent("ol", g)
        for k in range(2):
            sent("ir", g, k)
            sent("il", g, k)


def on_device(tokens, expert_ids, gate_weights, gate_up, down_proj):
    tok, width = tokens.shape
    top = expert_ids.shape[1]
    exp_dev, deep, _, ff = gate_up.shape
    cap = 9 * tok * top // (8 * exp_dev * N * N)
    half = N * cap
    rows = exp_dev * half
    route = jnp.concatenate([expert_ids.T.astype(F32), gate_weights.T], axis=0)
    flops = 2 * N * rows * deep * ff * 3
    n_copies = 5 * (N - 1) + 15 * N
    return pl.pallas_call(
        lambda *refs: kernel(cap, *refs),
        out_shape=jax.ShapeDtypeStruct((tok, width), BF16),
        in_specs=[pl.BlockSpec(memory_space=pltpu.VMEM)] * 2 + [pl.BlockSpec(memory_space=pl.ANY)] * 2,
        out_specs=pl.BlockSpec(memory_space=pltpu.VMEM),
        scratch_shapes=[
            pltpu.VMEM((2 * N, N, rows, width), BF16),
            pltpu.VMEM((N, N, rows, width), BF16),
            pltpu.VMEM((2, N, half, width), BF16),
            pltpu.VMEM((2, N, rows, width), BF16),
            pltpu.VMEM((N, rows, width), BF16),
            pltpu.VMEM((N - 1, rows, width), BF16),
            pltpu.VMEM((N, tok, width), BF16),
            pltpu.VMEM((N, 2 * top, tok), F32),
            pltpu.VMEM((N - 1, tok, width), BF16),
            pltpu.VMEM((N * tok, width), F32),
            pltpu.VMEM((rows, 2 * ff), F32),
            pltpu.VMEM((rows, ff), BF16),
            pltpu.VMEM((2 * N, N * tok), F32),
            pltpu.VMEM((2 * N, N * tok), F32),
            pltpu.VMEM((2 * N, exp_dev, width, 2 * ff), BF16),
            pltpu.VMEM((2 * N, exp_dev, ff, width), BF16),
            pltpu.SemaphoreType.DMA((4 * N,)),
            pltpu.SemaphoreType.DMA((n_copies,)),
            pltpu.SemaphoreType.DMA((n_copies,)),
        ],
        compiler_params=pltpu.CompilerParams(
            collective_id=0, has_side_effects=True, vmem_limit_bytes=60 << 20
        ),
        cost_estimate=pl.CostEstimate(flops=flops, bytes_accessed=24 << 20, transcendentals=0),
    )(tokens, route, gate_up.reshape(exp_dev, deep, 2 * ff), down_proj)


def solution(mesh):
    placed = (
        P("expert", "etensor"),
        P("expert", None),
        P("expert", None),
        P("expert", None, None, "etensor"),
        P("expert", "etensor", None),
    )
    return jax.shard_map(
        on_device, mesh=mesh, in_specs=placed, out_specs=P("expert", "etensor"), check_vma=False
    )
```

```python
import jax
import jax.numpy as jnp
from jax import lax
from jax.experimental import pallas as pl
from jax.experimental.pallas import tpu as pltpu
from jax.sharding import PartitionSpec as P

MESH = pl.DeviceIdType.MESH
F32, BF16 = jnp.float32, jnp.bfloat16
N = 4
SUB = 48


def dot(a, b):
    return jnp.dot(a, b, preferred_element_type=F32)


def kernel(cap, tokens, route, gate_up, down, out, X, SB, OP, IN, RET, PL, T, RT, ZR, CB, ACC, HID, SLOT, GATE,
           WG, WD, STAGE, wsem, gsem, ssem, rsem):
    half = N * cap
    rows = 2 * half
    top = route.shape[0] // 2
    tok, width = tokens.shape
    ff = down.shape[1]
    e, s = lax.axis_index("expert"), lax.axis_index("etensor")
    y, z, x, c = e // N, e % N, s // 2, s % 2

    def at_x(p, other):
        chip = (x + (0, N - 1, 1, 2)[p]) % N
        return chip * 2 + (1 - c if other else c)

    own, left, right, sibling = (e, s), (e, at_x(1, False)), (e, at_x(2, False)), (e, at_x(0, True))
    z_up = [(y * N + (z + d) % N, s) for d in range(N)]
    z_down = [(y * N + (z + N - d) % N, s) for d in range(N)]
    y_up = [((y + d) % N * N + z, s) for d in range(N)]
    y_down = [((y + N - d) % N * N + z, s) for d in range(N)]

    loads = []
    for q in range(2 * N):
        col = pl.multiple_of(at_x(q % N, q >= N) * width, 128)
        loads.append(pltpu.make_async_copy(down.at[:, :, pl.ds(col, width)], WD.at[q], wsem.at[q]))
    for load in loads:
        load.start()

    def stage_in(n):
        col = pl.multiple_of(at_x(n // 2 % N, n >= 2 * N) * width, 128)
        return pltpu.make_async_copy(gate_up.at[n % 2, pl.ds(col, width)], STAGE.at[n % 2], gsem.at[n % 2])

    def weights(first, last):
        for n in range(first, last):
            stage_in(n).wait()

            @pl.loop(0, width // tok)
            def _(i):
                at = pl.ds(pl.multiple_of(i * tok, tok), tok)
                WG[n // 2, n % 2, at, :] = STAGE[n % 2, at].reshape(tok, 2 * ff)

            if n + 2 < 4 * N:
                stage_in(n + 2).start()

    stage_in(0).start()
    stage_in(1).start()

    barrier = pltpu.get_barrier_semaphore()
    friends = z_up[1:] + y_up[1:] + [left, right, sibling]
    for f in friends:
        pl.semaphore_signal(barrier, inc=1, device_id=f, device_id_type=MESH)
    pl.semaphore_wait(barrier, len(friends))

    copies = {}

    def plan(key, src, dst, device):
        i = len(copies)
        copies[key] = pltpu.make_async_remote_copy(
            src_ref=src, dst_ref=dst, send_sem=ssem.at[i], recv_sem=rsem.at[i], device_id=device, device_id_type=MESH
        )

    lo, hi = pl.ds(0, half), pl.ds(half, half)
    for d in range(1, N):
        plan(("zt", d), tokens, T.at[d], z_up[d])
        plan(("zr", d), route, RT.at[d], z_up[d])
        plan(("zo", d), T.at[d], ZR.at[d - 1], z_down[d])
        plan(("yt", d), PL.at[d - 1], X.at[0, d], y_up[d])
        plan(("yo", d), X.at[0, d], RET.at[d], y_down[d])
    for g in range(N):
        plan(("r", g), X.at[0, g], X.at[1, g], right)
        plan(("l", g), X.at[0, g], X.at[2, g], left)
        plan(("rr", g), X.at[1, g, lo], X.at[3, g, lo], right)
        plan(("ll", g), X.at[2, g, hi], X.at[3, g, hi], left)
        for p in range(N):
            plan(("s", g, p), X.at[p, g], X.at[N + p, g], sibling)
        plan(("S", g), X.at[pl.ds(N, N), g], SB.at[:, g], sibling)
        plan(("or", g), X.at[3, g, lo], OP.at[0, g], right)
        plan(("ol", g), X.at[3, g, hi], OP.at[1, g], left)
        plan(("ir", g, 0), X.at[2, g, hi], IN.at[0, g, hi], right)
        plan(("il", g, 0), X.at[1, g, lo], IN.at[1, g, lo], left)
        plan(("ir", g, 1), X.at[2, g, lo], IN.at[0, g, lo], right)
        plan(("il", g, 1), X.at[1, g, hi], IN.at[1, g, hi], left)

    def start(*key):
        copies[key].start()

    def sent(*key):
        copies[key].wait_send()

    def got(*key):
        copies[key].wait_recv()

    for d in (1, 3, 2):
        start("zr", d)
        start("zt", d)

    T[0] = tokens[...]
    RT[0] = route[...]

    line = lax.broadcasted_iota(jnp.int32, (2 * N, tok), 0)
    expert = (2 * (N * ((y + line // 2) % N) + z) + line % 2).astype(F32)
    before = lax.broadcasted_iota(jnp.int32, (tok, tok), 0) < lax.broadcasted_iota(jnp.int32, (tok, tok), 1)
    before = jnp.where(before, 1.0, 0.0).astype(BF16)
    for d in range(N):
        if d:
            got("zr", d)
        named = jnp.zeros((2 * N, tok), F32)
        gate = jnp.zeros((2 * N, tok), F32)
        for k in range(top):
            hit = RT[d, k : k + 1, :] == expert
            named = named + jnp.where(hit, 1.0, 0.0)
            gate = gate + jnp.where(hit, RT[d, top + k : top + k + 1, :], 0.0)
        position = dot(named.astype(BF16), before)
        SLOT[:, d * tok : (d + 1) * tok] = jnp.where(named > 0.0, position + float(d * cap), -1.0)
        GATE[:, d * tok : (d + 1) * tok] = gate

    slot_of = lax.broadcasted_iota(jnp.int32, (half, N * tok), 0).astype(F32)

    def place(g, to):
        for j in range(2):
            i = 2 * g + j
            takes = jnp.where(slot_of == SLOT[i : i + 1, :], 1.0, 0.0).astype(BF16)
            to[j * half : (j + 1) * half, :] = dot(takes, T[...].reshape(N * tok, width)).astype(BF16)

    weights(0, 6)
    for d in range(1, N):
        got("zt", d)

    place(0, X.at[0, 0])

    def stage_a(g):
        if g:
            got("yt", g)
        start("r", g)
        start("l", g)
        start("s", g, 0)

    stage_a(0)
    for g in (1, 3, 2):
        place(g, PL.at[g - 1])
        start("yt", g)

    def stage_b(g):
        got("r", g)
        start("rr", g)
        got("l", g)
        start("ll", g)
        start("s", g, 1)
        start("s", g, 2)

    def stage_c(g):
        got("rr", g)
        got("ll", g)
        start("s", g, 3)

    def stage_d(g):
        for p in range(N):
            got("s", g, p)
        ACC[...] = jnp.zeros_like(ACC)

        @pl.loop(0, 2 * N)
        def _(q):
            for j in range(2):
                piece = pl.ds(j * half, half)
                ACC[piece, :] += dot(X[q, g, piece, :], WG[q, j])

        a = ACC[...]
        HID[...] = (jax.nn.silu(a[:, :ff]) * a[:, ff:]).astype(BF16)

        def down_of(q):
            for j in range(2):
                piece = pl.ds(j * half, half)
                X[q, g, piece, :] = dot(HID[piece, :], WD[q, j]).astype(BF16)

        pl.loop(N, 2 * N)(down_of)
        start("S", g)
        for k in ("r", "l", "rr", "ll"):
            sent(k, g)
        for p in range(N):
            sent("s", g, p)
        pl.loop(0, N)(down_of)

    def add(n, to, terms):
        @pl.loop(0, n // SUB)
        def _(i):
            at = pl.ds(pl.multiple_of(i * SUB, SUB), SUB)
            total = terms[0][at, :].astype(F32)
            for t in terms[1:]:
                total = total + t[at, :].astype(F32)
            to[at, :] = total.astype(BF16)

    def stage_e(g):
        got("S", g)
        add(rows, X.at[3, g], [X.at[3, g], SB.at[3, g]])
        start("or", g)
        start("ol", g)
        add(half, X.at[2, g, hi], [X.at[2, g, hi], SB.at[2, g, hi]])
        start("ir", g, 0)
        add(half, X.at[1, g, lo], [X.at[1, g, lo], SB.at[1, g, lo]])
        start("il", g, 0)

    def stage_f(g):
        got("or", g)
        add(half, X.at[2, g, lo], [X.at[2, g, lo], SB.at[2, g, lo], OP.at[0, g]])
        start("ir", g, 1)
        got("ol", g)
        add(half, X.at[1, g, hi], [X.at[1, g, hi], SB.at[1, g, hi], OP.at[1, g]])
        start("il", g, 1)

    def stage_g(g):
        for k in range(2):
            got("ir", g, k)
            got("il", g, k)
        add(rows, X.at[0, g] if g else RET.at[0], [X.at[0, g], SB.at[0, g], IN.at[0, g], IN.at[1, g]])
        if g:
            start("yo", g)

    def stage_h(g):
        if g:
            got("yo", g)
        for j in range(2):
            i = 2 * g + j
            takes = jnp.where(slot_of == SLOT[i : i + 1, :], GATE[i : i + 1, :], 0.0).astype(BF16)
            product = lax.dot_general(
                takes, RET[g, j * half : (j + 1) * half, :], (((0,), (0,)), ((), ())), preferred_element_type=F32
            )
            CB[...] = product if i == 0 else CB[...] + product

    weights(6, 9)
    stage_a(1)
    weights(9, 12)
    stage_b(0)
    weights(12, 14)
    stage_a(2)
    weights(14, 16)
    stage_b(1)
    for load in loads:
        load.wait()
    stage_c(0)
    stage_d(0)
    stage_a(3)
    stage_b(2)
    stage_e(0)
    stage_c(1)
    stage_d(1)
    stage_f(0)
    stage_b(3)
    stage_e(1)
    stage_c(2)
    stage_d(2)
    stage_g(0)
    stage_f(1)
    stage_e(2)
    stage_c(3)
    stage_d(3)
    stage_g(1)
    stage_f(2)
    stage_e(3)
    stage_h(0)
    stage_h(1)
    stage_g(2)
    stage_f(3)
    stage_h(2)
    stage_g(3)
    stage_h(3)
    for d in range(1, N):
        sent("zt", d)
        T[d] = CB[d * tok : (d + 1) * tok, :].astype(BF16)
        start("zo", d)
    total = CB[0:tok, :]
    for d in range(1, N):
        got("zo", d)
        total = total + ZR[d - 1].astype(F32)
    out[...] = total.astype(BF16)

    for d in range(1, N):
        for k in ("zr", "zo", "yt", "yo"):
            sent(k, d)
    for g in range(N):
        sent("S", g)
        sent("or", g)
        sent("ol", g)
        for k in range(2):
            sent("ir", g, k)
            sent("il", g, k)


def on_device(tokens, expert_ids, gate_weights, gate_up, down_proj):
    tok, width = tokens.shape
    top = expert_ids.shape[1]
    exp_dev, deep, _, ff = gate_up.shape
    cap = 9 * tok * top // (8 * exp_dev * N * N)
    half = N * cap
    rows = exp_dev * half
    route = jnp.concatenate([expert_ids.T.astype(F32), gate_weights.T], axis=0)
    flops = 2 * N * rows * deep * ff * 3
    n_copies = 5 * (N - 1) + 15 * N
    return pl.pallas_call(
        lambda *refs: kernel(cap, *refs),
        out_shape=jax.ShapeDtypeStruct((tok, width), BF16),
        in_specs=[pl.BlockSpec(memory_space=pltpu.VMEM)] * 2 + [pl.BlockSpec(memory_space=pl.ANY)] * 2,
        out_specs=pl.BlockSpec(memory_space=pltpu.VMEM),
        scratch_shapes=[
            pltpu.VMEM((2 * N, N, rows, width), BF16),
            pltpu.VMEM((N, N, rows, width), BF16),
            pltpu.VMEM((2, N, half, width), BF16),
            pltpu.VMEM((2, N, rows, width), BF16),
            pltpu.VMEM((N, rows, width), BF16),
            pltpu.VMEM((N - 1, rows, width), BF16),
            pltpu.VMEM((N, tok, width), BF16),
            pltpu.VMEM((N, 2 * top, tok), F32),
            pltpu.VMEM((N - 1, tok, width), BF16),
            pltpu.VMEM((N * tok, width), F32),
            pltpu.VMEM((rows, 2 * ff), F32),
            pltpu.VMEM((rows, ff), BF16),
            pltpu.VMEM((2 * N, N * tok), F32),
            pltpu.VMEM((2 * N, N * tok), F32),
            pltpu.VMEM((2 * N, exp_dev, width, 2 * ff), BF16),
            pltpu.VMEM((2 * N, exp_dev, ff, width), BF16),
            pltpu.VMEM((2, width, 2, ff), BF16),
            pltpu.SemaphoreType.DMA((2 * N,)),
            pltpu.SemaphoreType.DMA((2,)),
            pltpu.SemaphoreType.DMA((n_copies,)),
            pltpu.SemaphoreType.DMA((n_copies,)),
        ],
        compiler_params=pltpu.CompilerParams(
            collective_id=0, has_side_effects=True, vmem_limit_bytes=62 << 20
        ),
        cost_estimate=pl.CostEstimate(flops=flops, bytes_accessed=24 << 20, transcendentals=0),
    )(tokens, route, gate_up, down_proj)


def solution(mesh):
    placed = (
        P("expert", "etensor"),
        P("expert", None),
        P("expert", None),
        P("expert", None, None, "etensor"),
        P("expert", "etensor", None),
    )
    return jax.shard_map(
        on_device, mesh=mesh, in_specs=placed, out_specs=P("expert", "etensor"), check_vma=False
    )
```

```python
import jax
import jax.numpy as jnp
from jax import lax
from jax.experimental import pallas as pl
from jax.experimental.pallas import tpu as pltpu
from jax.sharding import PartitionSpec as P

MESH = pl.DeviceIdType.MESH
F32, BF16 = jnp.float32, jnp.bfloat16
N = 4
SUB = 48


def dot(a, b):
    return jnp.dot(a, b, preferred_element_type=F32)


def kernel(cap, a_cols, tokens, ids, gates, gate_up, down, out, XA, XB, SA, SB, OP, IN, PL, PA, T, TA, RT, ZR, ZA, XR, CB, CA, ACC, HID,
           SLOT, GATE, WG, WD, STAGE, free, wsem, gsem, ssem, rsem):
    half = N * cap
    rows = 2 * half
    top = ids.shape[0]
    tok, width = tokens.shape
    ff = down.shape[1]
    e, s = lax.axis_index("expert"), lax.axis_index("etensor")
    y, z, x, c = e // N, e % N, s // 2, s % 2
    A, B = pl.ds(0, a_cols), pl.ds(a_cols, width - a_cols)
    lo, hi = pl.ds(0, half), pl.ds(half, half)
    here, there = pl.ds(0, N), pl.ds(N, N)

    def at_x(p, other):
        chip = (x + (0, N - 1, 1, 2)[p]) % N
        return chip * 2 + (1 - c if other else c)

    x_at = [(e, at_x(p, False)) for p in range(N)]
    back = (0, 2, 1, 3)
    left, right, sibling = x_at[1], x_at[2], (e, at_x(0, True))
    z_up = [(y * N + (z + d) % N, s) for d in range(N)]
    z_down = [(y * N + (z + N - d) % N, s) for d in range(N)]
    y_up = [((y + d) % N * N + z, s) for d in range(N)]
    y_down = [((y + N - d) % N * N + z, s) for d in range(N)]

    def stage_in(n):
        col = pl.multiple_of(at_x(n // 2 % N, n >= 2 * N) * width, 128)
        return pltpu.make_async_copy(gate_up.at[n % 2, pl.ds(col, width)], STAGE.at[n % 2], gsem.at[n % 2])

    def weights(first, last):
        for n in range(first, last):
            stage_in(n).wait()

            @pl.loop(0, width // tok)
            def _(i):
                at = pl.ds(pl.multiple_of(i * tok, tok), tok)
                WG[n // 2, n % 2, at, :] = STAGE[n % 2, at].reshape(tok, 2 * ff)

            if n + 2 < 4 * N:
                stage_in(n + 2).start()

    stage_in(0).start()
    stage_in(1).start()
    loads = []
    for q in range(2 * N):
        col = pl.multiple_of(at_x(q % N, q >= N) * width, 128)
        loads.append(pltpu.make_async_copy(down.at[:, :, pl.ds(col, width)], WD.at[q], wsem.at[q]))
    for load in loads:
        load.start()

    RT[0, 0:top, :] = ids[...].astype(F32)
    RT[0, top : 2 * top, :] = gates[...]

    barrier = pltpu.get_barrier_semaphore()
    friends = z_up[1:] + y_up[1:] + x_at[1:] + [sibling]
    for f in friends:
        pl.semaphore_signal(barrier, inc=1, device_id=f, device_id_type=MESH)
    pl.semaphore_wait(barrier, len(friends))

    copies, done = {}, set()

    def plan(key, src, dst, device):
        i = len(copies)
        copies[key] = pltpu.make_async_remote_copy(
            src_ref=src, dst_ref=dst, send_sem=ssem.at[i], recv_sem=rsem.at[i], device_id=device, device_id_type=MESH
        )

    for p in range(1, N):
        plan(("xa", p), tokens.at[:, A], TA.at[0, back[p]], x_at[p])
        plan(("xo", p), TA.at[0, p], XR.at[back[p] - 1], x_at[p])
    for d in range(1, N):
        plan(("zt", d), tokens.at[:, B], T.at[d], z_up[d])
        plan(("zr", d), RT.at[0], RT.at[d], z_up[d])
        plan(("za", d), TA.at[0], TA.at[d], z_up[d])
        plan(("zo", d), T.at[d], ZR.at[d - 1], z_down[d])
        plan(("zoa", d), TA.at[d], ZA.at[d - 1], z_down[d])
        plan(("yt", d), PL.at[d - 1], XB.at[0, d], y_up[d])
        plan(("yo", d), XB.at[0, d], PL.at[d - 1], y_down[d])
        plan(("ta", d), PA.at[d - 1], XA.at[here, d], y_up[d])
        plan(("ya", d), XA.at[here, d], PA.at[d - 1], y_down[d])
    for g in range(N):
        plan(("r", g), XB.at[0, g], XB.at[1, g], right)
        plan(("l", g), XB.at[0, g], XB.at[2, g], left)
        plan(("rr", g), XB.at[1, g, lo], XB.at[3, g, lo], right)
        plan(("ll", g), XB.at[2, g, hi], XB.at[3, g, hi], left)
        for p in range(N):
            plan(("s", g, p), XB.at[p, g], XB.at[N + p, g], sibling)
        plan(("sa", g), XA.at[here, g], XA.at[there, g], sibling)
        plan(("SA", g), XA.at[there, g], SA.at[:, g], sibling)
        plan(("S", g), XB.at[there, g], SB.at[:, g], sibling)
        plan(("or", g), XB.at[3, g, lo], OP.at[0, g], right)
        plan(("ol", g), XB.at[3, g, hi], OP.at[1, g], left)
        plan(("ir", g, 0), XB.at[2, g, hi], IN.at[0, g, hi], right)
        plan(("il", g, 0), XB.at[1, g, lo], IN.at[1, g, lo], left)
        plan(("ir", g, 1), XB.at[2, g, lo], IN.at[0, g, lo], right)
        plan(("il", g, 1), XB.at[1, g, hi], IN.at[1, g, hi], left)

    def start(*key):
        copies[key].start()

    def sent(*key):
        if key not in done:
            done.add(key)
            copies[key].wait_send()

    def got(*key):
        copies[key].wait_recv()

    for d in (1, 3, 2):
        start("zr", d)
        start("zt", d)
    for p in range(1, N):
        start("xa", p)

    T[0] = tokens[:, B]
    TA[0, 0] = tokens[:, A]
    weights(0, 2)
    for p in range(1, N):
        got("xa", p)
    for d in (1, 3, 2):
        start("za", d)

    line = lax.broadcasted_iota(jnp.int32, (2 * N, tok), 0)
    expert = (2 * (N * ((y + line // 2) % N) + z) + line % 2).astype(F32)
    before = lax.broadcasted_iota(jnp.int32, (tok, tok), 0) < lax.broadcasted_iota(jnp.int32, (tok, tok), 1)
    before = jnp.where(before, 1.0, 0.0).astype(BF16)
    for d in range(N):
        if d:
            got("zr", d)
        named = jnp.zeros((2 * N, tok), F32)
        gate = jnp.zeros((2 * N, tok), F32)
        for k in range(top):
            hit = RT[d, k : k + 1, :] == expert
            named = named + jnp.where(hit, 1.0, 0.0)
            gate = gate + jnp.where(hit, RT[d, top + k : top + k + 1, :], 0.0)
        position = dot(named.astype(BF16), before)
        SLOT[:, d * tok : (d + 1) * tok] = jnp.where(named > 0.0, position + float(d * cap), -1.0)
        GATE[:, d * tok : (d + 1) * tok] = gate

    slot_of = lax.broadcasted_iota(jnp.int32, (half, N * tok), 0).astype(F32)

    def place(g, to):
        for j in range(2):
            i = 2 * g + j
            takes = jnp.where(slot_of == SLOT[i : i + 1, :], 1.0, 0.0).astype(BF16)
            for source, where in to:
                taken = dot(takes, source[...].reshape(N * tok, source.shape[-1]))
                where[j * half : (j + 1) * half, :] = taken.astype(BF16)

    weights(2, 5)
    for d in range(1, N):
        got("zt", d)

    place(0, [(T, XB.at[0, 0])])

    def stage_a(g):
        if g:
            got("yt", g)
        start("r", g)
        start("l", g)
        start("s", g, 0)

    stage_a(0)
    for g in (1, 3, 2):
        place(g, [(T, PL.at[g - 1])])
        start("yt", g)
    for d in range(1, N):
        got("za", d)
    for g in (1, 3, 2):
        place(g, [(TA.at[:, p], PA.at[g - 1, p]) for p in range(N)])
        start("ta", g)
    place(0, [(TA.at[:, p], XA.at[p, 0]) for p in range(N)])

    def stage_b(g):
        got("r", g)
        start("rr", g)
        got("l", g)
        start("ll", g)

    def stage_c(g):
        start("s", g, 1)
        start("s", g, 2)
        if g:
            got("ta", g)
        start("sa", g)
        got("rr", g)
        got("ll", g)
        start("s", g, 3)

    def stage_d(g):
        for p in range(N):
            got("s", g, p)
        got("sa", g)
        ACC[...] = jnp.zeros_like(ACC)

        @pl.loop(0, 2 * N)
        def _(q):
            for j in range(2):
                piece = pl.ds(j * half, half)
                ACC[piece, :] += dot(XB[q, g, piece, :], WG[q, j, B, :]) + dot(XA[q, g, piece, :], WG[q, j, A, :])

        acc = ACC[...]
        HID[...] = (jax.nn.silu(acc[:, :ff]) * acc[:, ff:]).astype(BF16)

        def down_of(q):
            for j in range(2):
                piece = pl.ds(j * half, half)
                result = dot(HID[piece, :], WD[q, j]).astype(BF16)
                XA[q, g, piece, :] = result[:, :a_cols]
                XB[q, g, piece, :] = result[:, a_cols:]

        pl.loop(N, 2 * N)(down_of)
        start("S", g)
        start("SA", g)
        for k in ("r", "l", "rr", "ll", "sa"):
            sent(k, g)
        for p in range(N):
            sent("s", g, p)
        pl.loop(0, N)(down_of)

    def add(n, to, terms):
        @pl.loop(0, n // SUB)
        def _(i):
            at = pl.ds(pl.multiple_of(i * SUB, SUB), SUB)
            total = terms[0][at, :].astype(F32)
            for t in terms[1:]:
                total = total + t[at, :].astype(F32)
            to[at, :] = total.astype(BF16)

    def sum_at(p, g, *more):
        add(rows, XB.at[p, g], [XB.at[p, g], SB.at[p, g], *more])

    def sum_part(p, g, part, *more):
        add(half, XB.at[p, g, part], [XB.at[p, g, part], SB.at[p, g, part], *more])

    def release(g):
        sent("yt", g)
        sent("ta", g)
        pl.semaphore_signal(free.at[g - 1], inc=1, device_id=y_up[g], device_id_type=MESH)

    def stage_e(g):
        got("S", g)
        sum_at(3, g)
        start("or", g)
        start("ol", g)
        sum_part(2, g, hi)
        start("ir", g, 0)
        sum_part(1, g, lo)
        start("il", g, 0)
        got("SA", g)
        for p in range(N):
            add(rows, XA.at[p, g], [XA.at[p, g], SA.at[p, g]])
        if g:
            pl.semaphore_wait(free.at[g - 1], 1)
            start("ya", g)

    def stage_f(g):
        got("or", g)
        sum_part(2, g, lo, OP.at[0, g])
        start("ir", g, 1)
        got("ol", g)
        sum_part(1, g, hi, OP.at[1, g])
        start("il", g, 1)

    def stage_g(g):
        for k in range(2):
            got("ir", g, k)
            got("il", g, k)
        sum_at(0, g, IN.at[0, g], IN.at[1, g])
        if g:
            start("yo", g)

    def combine(g, first, parts):
        @pl.loop(0, N)
        def _(d):
            at = pl.ds(pl.multiple_of(d * tok, tok), tok)
            for j in range(2):
                i = 2 * g + j
                slots = lax.broadcasted_iota(jnp.int32, (half, tok), 0).astype(F32)
                takes = jnp.where(slots == SLOT[i : i + 1, at], GATE[i : i + 1, at], 0.0).astype(BF16)
                for from_, total in parts:
                    product = lax.dot_general(
                        takes, from_[j * half : (j + 1) * half, :], (((0,), (0,)), ((), ())), preferred_element_type=F32
                    )
                    total[at, :] = product if first and j == 0 else total[at, :] + product

    def stage_h(g, first=False):
        if g:
            got("yo", g)
        combine(g, first, [(PL.at[g - 1] if g else XB.at[0, 0], CB)])

    def stage_ha(g, first=False):
        if g:
            got("ya", g)
        combine(g, first, [(PA.at[g - 1, p] if g else XA.at[p, 0], CA.at[p]) for p in range(N)])

    weights(5, 8)
    stage_b(0)
    weights(8, 10)
    stage_a(1)
    stage_a(3)
    stage_c(0)
    weights(10, 14)
    stage_b(1)
    stage_a(2)
    weights(14, 16)
    for load in loads:
        load.wait()
    stage_b(3)
    stage_c(1)
    stage_d(1)
    for g in (1, 3, 2):
        release(g)
    stage_c(3)
    stage_b(2)
    stage_e(1)
    stage_d(3)
    stage_f(1)
    stage_c(2)
    stage_e(3)
    stage_d(2)
    stage_g(1)
    stage_f(3)
    stage_e(2)
    stage_d(0)
    stage_g(3)
    stage_f(2)
    stage_e(0)
    stage_ha(1, True)
    stage_ha(3)
    stage_g(2)
    stage_f(0)
    stage_ha(2)
    stage_ha(0)
    for d in range(1, N):
        sent("za", d)
    for d in range(1, N):
        TA[d] = CA[:, d * tok : (d + 1) * tok, :].astype(BF16)
        start("zoa", d)
    stage_h(1, True)
    stage_h(3)
    total = CA[:, 0:tok, :]
    for d in range(1, N):
        got("zoa", d)
        total = total + ZA[d - 1].astype(F32)
    CA[0, 0:tok, :] = total[0]
    TA[0] = total.astype(BF16)
    for p in range(1, N):
        start("xo", p)
    stage_h(2)
    stage_g(0)
    stage_h(0)
    for d in range(1, N):
        sent("zt", d)
        T[d] = CB[d * tok : (d + 1) * tok, :].astype(BF16)
        start("zo", d)
    total = CA[0, 0:tok, :]
    for p in range(1, N):
        got("xo", p)
        total = total + XR[back[p] - 1].astype(F32)
    out[:, A] = total.astype(BF16)
    total = CB[0:tok, :]
    for d in range(1, N):
        got("zo", d)
        total = total + ZR[d - 1].astype(F32)
    out[:, B] = total.astype(BF16)
    for key in copies:
        sent(*key)


def on_device(tokens, expert_ids, gate_weights, gate_up, down_proj):
    tok, width = tokens.shape
    top = expert_ids.shape[1]
    exp_dev, deep, _, ff = gate_up.shape
    cap = 9 * tok * top // (8 * exp_dev * N * N)
    half = N * cap
    rows = exp_dev * half
    a_cols = 256
    b_cols = width - a_cols
    flops = 2 * N * rows * deep * ff * 3
    n_copies = 11 * (N - 1) + 17 * N
    return pl.pallas_call(
        lambda *refs: kernel(cap, a_cols, *refs),
        out_shape=jax.ShapeDtypeStruct((tok, width), BF16),
        in_specs=[pl.BlockSpec(memory_space=pltpu.VMEM)] * 3 + [pl.BlockSpec(memory_space=pl.ANY)] * 2,
        out_specs=pl.BlockSpec(memory_space=pltpu.VMEM),
        scratch_shapes=[
            pltpu.VMEM((2 * N, N, rows, a_cols), BF16),
            pltpu.VMEM((2 * N, N, rows, b_cols), BF16),
            pltpu.VMEM((N, N, rows, a_cols), BF16),
            pltpu.VMEM((N, N, rows, b_cols), BF16),
            pltpu.VMEM((2, N, half, b_cols), BF16),
            pltpu.VMEM((2, N, rows, b_cols), BF16),
            pltpu.VMEM((N - 1, rows, b_cols), BF16),
            pltpu.VMEM((N - 1, N, rows, a_cols), BF16),
            pltpu.VMEM((N, tok, b_cols), BF16),
            pltpu.VMEM((N, N, tok, a_cols), BF16),
            pltpu.VMEM((N, 2 * top, tok), F32),
            pltpu.VMEM((N - 1, tok, b_cols), BF16),
            pltpu.VMEM((N - 1, N, tok, a_cols), BF16),
            pltpu.VMEM((N - 1, tok, a_cols), BF16),
            pltpu.VMEM((N * tok, b_cols), F32),
            pltpu.VMEM((N, N * tok, a_cols), F32),
            pltpu.VMEM((rows, 2 * ff), F32),
            pltpu.VMEM((rows, ff), BF16),
            pltpu.VMEM((2 * N, N * tok), F32),
            pltpu.VMEM((2 * N, N * tok), F32),
            pltpu.VMEM((2 * N, exp_dev, width, 2 * ff), BF16),
            pltpu.VMEM((2 * N, exp_dev, ff, width), BF16),
            pltpu.VMEM((2, width, 2, ff), BF16),
            pltpu.SemaphoreType.REGULAR((N - 1,)),
            pltpu.SemaphoreType.DMA((2 * N,)),
            pltpu.SemaphoreType.DMA((2,)),
            pltpu.SemaphoreType.DMA((n_copies,)),
            pltpu.SemaphoreType.DMA((n_copies,)),
        ],
        compiler_params=pltpu.CompilerParams(
            collective_id=0, has_side_effects=True, vmem_limit_bytes=62 << 20
        ),
        cost_estimate=pl.CostEstimate(flops=flops, bytes_accessed=24 << 20, transcendentals=0),
    )(tokens, expert_ids.T, gate_weights.T, gate_up, down_proj)


def solution(mesh):
    placed = (
        P("expert", "etensor"),
        P("expert", None),
        P("expert", None),
        P("expert", None, None, "etensor"),
        P("expert", "etensor", None),
    )
    return jax.shard_map(
        on_device, mesh=mesh, in_specs=placed, out_specs=P("expert", "etensor"), check_vma=False
    )
```

```python
import jax
import jax.numpy as jnp
from jax import lax
from jax.experimental import pallas as pl
from jax.experimental.pallas import tpu as pltpu
from jax.sharding import PartitionSpec as P

MESH = pl.DeviceIdType.MESH
F32, BF16 = jnp.float32, jnp.bfloat16
N = 4
SUB = 48


def dot(a, b):
    return jnp.dot(a, b, preferred_element_type=F32)


def kernel(cap, a_cols, tokens, ids, gates, gate_up, down, out, XA, XB, SA, SB, OP, IN, PL, PA, T, TA, RT, ZR, ZA, XR, CB, CA, ACC, HID,
           SLOT, GATE, WG, WD, STAGE, free, wsem, gsem, ssem, rsem):
    half = N * cap
    rows = 2 * half
    top = ids.shape[0]
    tok, width = tokens.shape
    ff = down.shape[1]
    e, s = lax.axis_index("expert"), lax.axis_index("etensor")
    y, z, x, c = e // N, e % N, s // 2, s % 2
    A, B = pl.ds(0, a_cols), pl.ds(a_cols, width - a_cols)
    lo, hi = pl.ds(0, half), pl.ds(half, half)
    here, there = pl.ds(0, N), pl.ds(N, N)

    def at_x(p, other):
        chip = (x + (0, N - 1, 1, 2)[p]) % N
        return chip * 2 + (1 - c if other else c)

    x_at = [(e, at_x(p, False)) for p in range(N)]
    back = (0, 2, 1, 3)
    left, right, sibling = x_at[1], x_at[2], (e, at_x(0, True))
    z_up = [(y * N + (z + d) % N, s) for d in range(N)]
    z_down = [(y * N + (z + N - d) % N, s) for d in range(N)]
    y_up = [((y + d) % N * N + z, s) for d in range(N)]
    y_down = [((y + N - d) % N * N + z, s) for d in range(N)]

    def stage_in(n):
        col = pl.multiple_of(at_x(n // 2 % N, n >= 2 * N) * width, 128)
        return pltpu.make_async_copy(gate_up.at[n % 2, pl.ds(col, width)], STAGE.at[n % 2], gsem.at[n % 2])

    def weights(first, last):
        for n in range(first, last):
            stage_in(n).wait()

            @pl.loop(0, width // tok)
            def _(i):
                at = pl.ds(pl.multiple_of(i * tok, tok), tok)
                WG[n // 2, n % 2, at, :] = STAGE[n % 2, at].reshape(tok, 2 * ff)

            if n + 2 < 4 * N:
                stage_in(n + 2).start()

    stage_in(0).start()
    stage_in(1).start()
    loads = []
    for q in range(2 * N):
        col = pl.multiple_of(at_x(q % N, q >= N) * width, 128)
        loads.append(pltpu.make_async_copy(down.at[:, :, pl.ds(col, width)], WD.at[q], wsem.at[q]))
    for load in loads:
        load.start()

    RT[0, 0:top, :] = ids[...].astype(F32)
    RT[0, top : 2 * top, :] = gates[...]

    barrier = pltpu.get_barrier_semaphore()
    friends = z_up[1:] + y_up[1:] + x_at[1:] + [sibling]
    for f in friends:
        pl.semaphore_signal(barrier, inc=1, device_id=f, device_id_type=MESH)
    pl.semaphore_wait(barrier, len(friends))

    copies, done = {}, set()

    def plan(key, src, dst, device):
        i = len(copies)
        copies[key] = pltpu.make_async_remote_copy(
            src_ref=src, dst_ref=dst, send_sem=ssem.at[i], recv_sem=rsem.at[i], device_id=device, device_id_type=MESH
        )

    for p in range(1, N):
        plan(("xa", p), tokens.at[:, A], TA.at[0, back[p]], x_at[p])
        plan(("xo", p), TA.at[0, p], XR.at[back[p] - 1], x_at[p])
    for d in range(1, N):
        plan(("zt", d), tokens.at[:, B], T.at[d], z_up[d])
        plan(("zr", d), RT.at[0], RT.at[d], z_up[d])
        plan(("za", d), TA.at[0], TA.at[d], z_up[d])
        plan(("zo", d), T.at[d], ZR.at[d - 1], z_down[d])
        plan(("zoa", d), TA.at[d], ZA.at[d - 1], z_down[d])
        plan(("yt", d), PL.at[d - 1], XB.at[0, d], y_up[d])
        plan(("yo", d), XB.at[0, d], PL.at[d - 1], y_down[d])
        plan(("ta", d), PA.at[d - 1], XA.at[here, d], y_up[d])
        plan(("ya", d), XA.at[here, d], PA.at[d - 1], y_down[d])
    for g in range(N):
        plan(("r", g), XB.at[0, g], XB.at[1, g], right)
        plan(("l", g), XB.at[0, g], XB.at[2, g], left)
        plan(("rr", g), XB.at[1, g, lo], XB.at[3, g, lo], right)
        plan(("ll", g), XB.at[2, g, hi], XB.at[3, g, hi], left)
        for p in range(N):
            plan(("s", g, p), XB.at[p, g], XB.at[N + p, g], sibling)
        plan(("sa", g), XA.at[here, g], XA.at[there, g], sibling)
        plan(("SA", g), XA.at[there, g], SA.at[:, g], sibling)
        plan(("S", g), XB.at[there, g], SB.at[:, g], sibling)
        plan(("or", g), XB.at[3, g, lo], OP.at[0, g], right)
        plan(("ol", g), XB.at[3, g, hi], OP.at[1, g], left)
        plan(("ir", g, 0), XB.at[2, g, hi], IN.at[0, g, hi], right)
        plan(("il", g, 0), XB.at[1, g, lo], IN.at[1, g, lo], left)
        plan(("ir", g, 1), XB.at[2, g, lo], IN.at[0, g, lo], right)
        plan(("il", g, 1), XB.at[1, g, hi], IN.at[1, g, hi], left)

    def start(*key):
        copies[key].start()

    def sent(*key):
        if key not in done:
            done.add(key)
            copies[key].wait_send()

    def got(*key):
        copies[key].wait_recv()

    for d in (1, 3, 2):
        start("zr", d)
        start("zt", d)
    for p in range(1, N):
        start("xa", p)

    T[0] = tokens[:, B]
    TA[0, 0] = tokens[:, A]
    weights(0, 2)

    line = lax.broadcasted_iota(jnp.int32, (2 * N, tok), 0)
    expert = (2 * (N * ((y + line // 2) % N) + z) + line % 2).astype(F32)
    before = lax.broadcasted_iota(jnp.int32, (tok, tok), 0) < lax.broadcasted_iota(jnp.int32, (tok, tok), 1)
    before = jnp.where(before, 1.0, 0.0).astype(BF16)
    for d in range(N):
        if d:
            got("zr", d)
        named = jnp.zeros((2 * N, tok), F32)
        gate = jnp.zeros((2 * N, tok), F32)
        for k in range(top):
            hit = RT[d, k : k + 1, :] == expert
            named = named + jnp.where(hit, 1.0, 0.0)
            gate = gate + jnp.where(hit, RT[d, top + k : top + k + 1, :], 0.0)
        position = dot(named.astype(BF16), before)
        SLOT[:, d * tok : (d + 1) * tok] = jnp.where(named > 0.0, position + float(d * cap), -1.0)
        GATE[:, d * tok : (d + 1) * tok] = gate

    slot_of = lax.broadcasted_iota(jnp.int32, (half, N * tok), 0).astype(F32)

    def place(g, to):
        for j in range(2):
            i = 2 * g + j
            takes = jnp.where(slot_of == SLOT[i : i + 1, :], 1.0, 0.0).astype(BF16)
            for source, where in to:
                taken = dot(takes, source[...].reshape(N * tok, source.shape[-1]))
                where[j * half : (j + 1) * half, :] = taken.astype(BF16)

    weights(2, 5)
    for d in range(1, N):
        got("zt", d)
    for p in range(1, N):
        got("xa", p)
    for d in (1, 3, 2):
        start("za", d)

    place(0, [(T, XB.at[0, 0])])

    def stage_a(g):
        if g:
            got("yt", g)
        start("r", g)
        start("l", g)
        start("s", g, 0)

    stage_a(0)
    for g in (1, 3, 2):
        place(g, [(T, PL.at[g - 1])])
        start("yt", g)

    def stage_b(g):
        got("r", g)
        start("rr", g)
        got("l", g)
        start("ll", g)

    def stage_c(g):
        start("s", g, 1)
        start("s", g, 2)
        if g:
            got("ta", g)
        start("sa", g)
        got("rr", g)
        got("ll", g)
        start("s", g, 3)

    def stage_d(g):
        for p in range(N):
            got("s", g, p)
        got("sa", g)
        ACC[...] = jnp.zeros_like(ACC)

        @pl.loop(0, 2 * N)
        def _(q):
            for j in range(2):
                piece = pl.ds(j * half, half)
                ACC[piece, :] += dot(XB[q, g, piece, :], WG[q, j, B, :]) + dot(XA[q, g, piece, :], WG[q, j, A, :])

        acc = ACC[...]
        HID[...] = (jax.nn.silu(acc[:, :ff]) * acc[:, ff:]).astype(BF16)

        def down_of(q):
            for j in range(2):
                piece = pl.ds(j * half, half)
                result = dot(HID[piece, :], WD[q, j]).astype(BF16)
                XA[q, g, piece, :] = result[:, :a_cols]
                XB[q, g, piece, :] = result[:, a_cols:]

        pl.loop(N, 2 * N)(down_of)
        start("S", g)
        start("SA", g)
        for k in ("r", "l", "rr", "ll", "sa"):
            sent(k, g)
        for p in range(N):
            sent("s", g, p)
        pl.loop(0, N)(down_of)

    def add(n, to, terms):
        @pl.loop(0, n // SUB)
        def _(i):
            at = pl.ds(pl.multiple_of(i * SUB, SUB), SUB)
            total = terms[0][at, :].astype(F32)
            for t in terms[1:]:
                total = total + t[at, :].astype(F32)
            to[at, :] = total.astype(BF16)

    def sum_at(p, g, *more):
        add(rows, XB.at[p, g], [XB.at[p, g], SB.at[p, g], *more])

    def sum_part(p, g, part, *more):
        add(half, XB.at[p, g, part], [XB.at[p, g, part], SB.at[p, g, part], *more])

    def release(g):
        sent("yt", g)
        sent("ta", g)
        pl.semaphore_signal(free.at[g - 1], inc=1, device_id=y_up[g], device_id_type=MESH)

    def stage_e(g):
        got("S", g)
        sum_at(3, g)
        start("or", g)
        start("ol", g)
        sum_part(2, g, hi)
        start("ir", g, 0)
        sum_part(1, g, lo)
        start("il", g, 0)
        got("SA", g)
        for p in range(N):
            add(rows, XA.at[p, g], [XA.at[p, g], SA.at[p, g]])
        if g:
            pl.semaphore_wait(free.at[g - 1], 1)
            start("ya", g)

    def stage_f(g):
        got("or", g)
        sum_part(2, g, lo, OP.at[0, g])
        start("ir", g, 1)
        got("ol", g)
        sum_part(1, g, hi, OP.at[1, g])
        start("il", g, 1)

    def stage_g(g):
        for k in range(2):
            got("ir", g, k)
            got("il", g, k)
        sum_at(0, g, IN.at[0, g], IN.at[1, g])
        if g:
            start("yo", g)

    def combine(g, first, parts):
        @pl.loop(0, N)
        def _(d):
            at = pl.ds(pl.multiple_of(d * tok, tok), tok)
            for j in range(2):
                i = 2 * g + j
                slots = lax.broadcasted_iota(jnp.int32, (half, tok), 0).astype(F32)
                takes = jnp.where(slots == SLOT[i : i + 1, at], GATE[i : i + 1, at], 0.0).astype(BF16)
                for from_, total in parts:
                    product = lax.dot_general(
                        takes, from_[j * half : (j + 1) * half, :], (((0,), (0,)), ((), ())), preferred_element_type=F32
                    )
                    total[at, :] = product if first and j == 0 else total[at, :] + product

    def stage_h(g, first=False):
        if g:
            got("yo", g)
        combine(g, first, [(PL.at[g - 1] if g else XB.at[0, 0], CB)])

    def stage_ha(g, first=False):
        if g:
            got("ya", g)
        combine(g, first, [(PA.at[g - 1, p] if g else XA.at[p, 0], CA.at[p]) for p in range(N)])

    weights(5, 10)
    stage_b(0)
    stage_a(1)
    stage_a(3)
    for d in range(1, N):
        got("za", d)
    for g in (1, 3, 2):
        place(g, [(TA.at[:, p], PA.at[g - 1, p]) for p in range(N)])
        start("ta", g)
    place(0, [(TA.at[:, p], XA.at[p, 0]) for p in range(N)])
    stage_c(0)
    weights(10, 13)
    stage_b(1)
    stage_a(2)
    weights(13, 16)
    for load in loads:
        load.wait()
    stage_b(3)
    stage_c(1)
    stage_d(1)
    for g in (1, 3, 2):
        release(g)
    stage_c(3)
    stage_b(2)
    stage_e(1)
    stage_d(3)
    stage_f(1)
    stage_c(2)
    stage_e(3)
    stage_d(2)
    stage_g(1)
    stage_f(3)
    stage_e(2)
    stage_d(0)
    stage_g(3)
    stage_f(2)
    stage_ha(1, True)
    stage_ha(3)
    stage_e(0)
    stage_ha(2)
    stage_ha(0)
    for d in range(1, N):
        sent("za", d)
    for d in (1, 3, 2):
        TA[d] = CA[:, d * tok : (d + 1) * tok, :].astype(BF16)
        start("zoa", d)
    stage_h(1, True)
    stage_f(0)
    stage_g(2)
    stage_h(3)
    stage_h(2)
    stage_g(0)
    stage_h(0)
    for d in (1, 3, 2):
        T[d] = CB[d * tok : (d + 1) * tok, :].astype(BF16)
        start("zo", d)
    total = CA[:, 0:tok, :]
    for d in range(1, N):
        got("zoa", d)
        total = total + ZA[d - 1].astype(F32)
    CA[0, 0:tok, :] = total[0]
    TA[0] = total.astype(BF16)
    for p in range(1, N):
        start("xo", p)
    total = CB[0:tok, :]
    for d in range(1, N):
        got("zo", d)
        total = total + ZR[d - 1].astype(F32)
    out[:, B] = total.astype(BF16)
    total = CA[0, 0:tok, :]
    for p in range(1, N):
        got("xo", p)
        total = total + XR[back[p] - 1].astype(F32)
    out[:, A] = total.astype(BF16)
    for key in copies:
        sent(*key)


def on_device(tokens, expert_ids, gate_weights, gate_up, down_proj):
    tok, width = tokens.shape
    top = expert_ids.shape[1]
    exp_dev, deep, _, ff = gate_up.shape
    cap = 9 * tok * top // (8 * exp_dev * N * N)
    half = N * cap
    rows = exp_dev * half
    a_cols = 256
    b_cols = width - a_cols
    flops = 2 * N * rows * deep * ff * 3
    n_copies = 11 * (N - 1) + 17 * N
    return pl.pallas_call(
        lambda *refs: kernel(cap, a_cols, *refs),
        out_shape=jax.ShapeDtypeStruct((tok, width), BF16),
        in_specs=[pl.BlockSpec(memory_space=pltpu.VMEM)] * 3 + [pl.BlockSpec(memory_space=pl.ANY)] * 2,
        out_specs=pl.BlockSpec(memory_space=pltpu.VMEM),
        scratch_shapes=[
            pltpu.VMEM((2 * N, N, rows, a_cols), BF16),
            pltpu.VMEM((2 * N, N, rows, b_cols), BF16),
            pltpu.VMEM((N, N, rows, a_cols), BF16),
            pltpu.VMEM((N, N, rows, b_cols), BF16),
            pltpu.VMEM((2, N, half, b_cols), BF16),
            pltpu.VMEM((2, N, rows, b_cols), BF16),
            pltpu.VMEM((N - 1, rows, b_cols), BF16),
            pltpu.VMEM((N - 1, N, rows, a_cols), BF16),
            pltpu.VMEM((N, tok, b_cols), BF16),
            pltpu.VMEM((N, N, tok, a_cols), BF16),
            pltpu.VMEM((N, 2 * top, tok), F32),
            pltpu.VMEM((N - 1, tok, b_cols), BF16),
            pltpu.VMEM((N - 1, N, tok, a_cols), BF16),
            pltpu.VMEM((N - 1, tok, a_cols), BF16),
            pltpu.VMEM((N * tok, b_cols), F32),
            pltpu.VMEM((N, N * tok, a_cols), F32),
            pltpu.VMEM((rows, 2 * ff), F32),
            pltpu.VMEM((rows, ff), BF16),
            pltpu.VMEM((2 * N, N * tok), F32),
            pltpu.VMEM((2 * N, N * tok), F32),
            pltpu.VMEM((2 * N, exp_dev, width, 2 * ff), BF16),
            pltpu.VMEM((2 * N, exp_dev, ff, width), BF16),
            pltpu.VMEM((2, width, 2, ff), BF16),
            pltpu.SemaphoreType.REGULAR((N - 1,)),
            pltpu.SemaphoreType.DMA((2 * N,)),
            pltpu.SemaphoreType.DMA((2,)),
            pltpu.SemaphoreType.DMA((n_copies,)),
            pltpu.SemaphoreType.DMA((n_copies,)),
        ],
        compiler_params=pltpu.CompilerParams(
            collective_id=0, has_side_effects=True, vmem_limit_bytes=62 << 20
        ),
        cost_estimate=pl.CostEstimate(flops=flops, bytes_accessed=24 << 20, transcendentals=0),
    )(tokens, expert_ids.T, gate_weights.T, gate_up, down_proj)


def solution(mesh):
    placed = (
        P("expert", "etensor"),
        P("expert", None),
        P("expert", None),
        P("expert", None, None, "etensor"),
        P("expert", "etensor", None),
    )
    return jax.shard_map(
        on_device, mesh=mesh, in_specs=placed, out_specs=P("expert", "etensor"), check_vma=False
    )
```

```python
import jax
import jax.numpy as jnp
from jax import lax
from jax.experimental import pallas as pl
from jax.experimental.pallas import tpu as pltpu
from jax.sharding import PartitionSpec as P

MESH = pl.DeviceIdType.MESH
F32, BF16 = jnp.float32, jnp.bfloat16
N = 4
SUB = 48


def dot(a, b):
    return jnp.dot(a, b, preferred_element_type=F32)


def kernel(cap, a_cols, tokens, ids, gates, gate_up, down, out, XA, XB, SA, SB, OP, IN, PL, PA, T, TA, RT, ZR, ZA, XR, CB, CA, ACC, HID,
           SLOT, GATE, WG, WD, STAGE, free, wsem, gsem, ssem, rsem):
    half = N * cap
    rows = 2 * half
    top = ids.shape[0]
    tok, width = tokens.shape
    ff = down.shape[1]
    e, s = lax.axis_index("expert"), lax.axis_index("etensor")
    y, z, x, c = e // N, e % N, s // 2, s % 2
    A, B = pl.ds(0, a_cols), pl.ds(a_cols, width - a_cols)
    lo, hi = pl.ds(0, half), pl.ds(half, half)
    here, there = pl.ds(0, N), pl.ds(N, N)

    def at_x(p, other):
        chip = (x + (0, N - 1, 1, 2)[p]) % N
        return chip * 2 + (1 - c if other else c)

    x_at = [(e, at_x(p, False)) for p in range(N)]
    back = (0, 2, 1, 3)
    left, right, sibling = x_at[1], x_at[2], (e, at_x(0, True))
    z_up = [(y * N + (z + d) % N, s) for d in range(N)]
    z_down = [(y * N + (z + N - d) % N, s) for d in range(N)]
    y_up = [((y + d) % N * N + z, s) for d in range(N)]
    y_down = [((y + N - d) % N * N + z, s) for d in range(N)]

    def stage_in(n):
        col = pl.multiple_of(at_x(n // 2 % N, n >= 2 * N) * width, 128)
        return pltpu.make_async_copy(gate_up.at[n % 2, pl.ds(col, width)], STAGE.at[n % 2], gsem.at[n % 2])

    def weights(first, last):
        for n in range(first, last):
            stage_in(n).wait()

            @pl.loop(0, width // tok)
            def _(i):
                at = pl.ds(pl.multiple_of(i * tok, tok), tok)
                WG[n // 2, n % 2, at, :] = STAGE[n % 2, at].reshape(tok, 2 * ff)

            if n + 2 < 4 * N:
                stage_in(n + 2).start()

    stage_in(0).start()
    stage_in(1).start()
    loads = []
    for q in range(2 * N):
        col = pl.multiple_of(at_x(q % N, q >= N) * width, 128)
        loads.append(pltpu.make_async_copy(down.at[:, :, pl.ds(col, width)], WD.at[q], wsem.at[q]))
    for load in loads:
        load.start()

    RT[0, 0:top, :] = ids[...].astype(F32)
    RT[0, top : 2 * top, :] = gates[...]

    barrier = pltpu.get_barrier_semaphore()
    friends = z_up[1:] + y_up[1:] + x_at[1:] + [sibling]
    for f in friends:
        pl.semaphore_signal(barrier, inc=1, device_id=f, device_id_type=MESH)
    pl.semaphore_wait(barrier, len(friends))

    copies, done = {}, set()

    def plan(key, src, dst, device):
        i = len(copies)
        copies[key] = pltpu.make_async_remote_copy(
            src_ref=src, dst_ref=dst, send_sem=ssem.at[i], recv_sem=rsem.at[i], device_id=device, device_id_type=MESH
        )

    for p in range(1, N):
        plan(("xa", p), tokens.at[:, A], TA.at[0, back[p]], x_at[p])
        plan(("xo", p), TA.at[0, p], XR.at[back[p] - 1], x_at[p])
    for d in range(1, N):
        plan(("zt", d), tokens.at[:, B], T.at[d], z_up[d])
        plan(("zr", d), RT.at[0], RT.at[d], z_up[d])
        plan(("za", d), TA.at[0], TA.at[d], z_up[d])
        plan(("zo", d), T.at[d], ZR.at[d - 1], z_down[d])
        plan(("zoa", d), TA.at[d], ZA.at[d - 1], z_down[d])
        plan(("yt", d), PL.at[d - 1], XB.at[0, d], y_up[d])
        plan(("yo", d), XB.at[0, d], PL.at[d - 1], y_down[d])
        plan(("ta", d), PA.at[d - 1], XA.at[here, d], y_up[d])
        plan(("ya", d), XA.at[here, d], PA.at[d - 1], y_down[d])
    for g in range(N):
        plan(("r", g), XB.at[0, g], XB.at[1, g], right)
        plan(("l", g), XB.at[0, g], XB.at[2, g], left)
        plan(("rr", g), XB.at[1, g, lo], XB.at[3, g, lo], right)
        plan(("ll", g), XB.at[2, g, hi], XB.at[3, g, hi], left)
        for p in range(N):
            plan(("s", g, p), XB.at[p, g], XB.at[N + p, g], sibling)
        plan(("sa", g), XA.at[here, g], XA.at[there, g], sibling)
        plan(("SA", g), XA.at[there, g], SA.at[:, g], sibling)
        plan(("S", g), XB.at[there, g], SB.at[:, g], sibling)
        plan(("or", g), XB.at[3, g, lo], OP.at[0, g], right)
        plan(("ol", g), XB.at[3, g, hi], OP.at[1, g], left)
        plan(("ir", g, 0), XB.at[2, g, hi], IN.at[0, g, hi], right)
        plan(("il", g, 0), XB.at[1, g, lo], IN.at[1, g, lo], left)
        plan(("ir", g, 1), XB.at[2, g, lo], IN.at[0, g, lo], right)
        plan(("il", g, 1), XB.at[1, g, hi], IN.at[1, g, hi], left)

    def start(*key):
        copies[key].start()

    def sent(*key):
        if key not in done:
            done.add(key)
            copies[key].wait_send()

    def got(*key):
        copies[key].wait_recv()

    for d in (1, 3, 2):
        start("zr", d)
        start("zt", d)
    for p in range(1, N):
        start("xa", p)

    T[0] = tokens[:, B]
    TA[0, 0] = tokens[:, A]
    weights(0, 2)

    line = lax.broadcasted_iota(jnp.int32, (2 * N, tok), 0)
    expert = (2 * (N * ((y + line // 2) % N) + z) + line % 2).astype(F32)
    before = lax.broadcasted_iota(jnp.int32, (tok, tok), 0) < lax.broadcasted_iota(jnp.int32, (tok, tok), 1)
    before = jnp.where(before, 1.0, 0.0).astype(BF16)
    for d in range(N):
        if d:
            got("zr", d)
        named = jnp.zeros((2 * N, tok), F32)
        gate = jnp.zeros((2 * N, tok), F32)
        for k in range(top):
            hit = RT[d, k : k + 1, :] == expert
            named = named + jnp.where(hit, 1.0, 0.0)
            gate = gate + jnp.where(hit, RT[d, top + k : top + k + 1, :], 0.0)
        position = dot(named.astype(BF16), before)
        SLOT[:, d * tok : (d + 1) * tok] = jnp.where(named > 0.0, position + float(d * cap), -1.0)
        GATE[:, d * tok : (d + 1) * tok] = gate

    slot_of = lax.broadcasted_iota(jnp.int32, (half, N * tok), 0).astype(F32)

    def place(g, to):
        for j in range(2):
            i = 2 * g + j
            takes = jnp.where(slot_of == SLOT[i : i + 1, :], 1.0, 0.0).astype(BF16)
            for source, where in to:
                taken = dot(takes, source[...].reshape(N * tok, source.shape[-1]))
                where[j * half : (j + 1) * half, :] = taken.astype(BF16)

    weights(2, 5)
    for d in range(1, N):
        got("zt", d)
    for p in range(1, N):
        got("xa", p)
    for d in (1, 3, 2):
        start("za", d)

    place(0, [(T, XB.at[0, 0])])

    def stage_a(g):
        if g:
            got("yt", g)
        start("r", g)
        start("l", g)
        start("s", g, 0)

    stage_a(0)
    for g in (1, 3, 2):
        place(g, [(T, PL.at[g - 1])])
        start("yt", g)

    def stage_b(g):
        got("r", g)
        start("rr", g)
        got("l", g)
        start("ll", g)

    def stage_c(g):
        start("s", g, 1)
        start("s", g, 2)
        if g:
            got("ta", g)
        start("sa", g)
        got("rr", g)
        got("ll", g)
        start("s", g, 3)

    def stage_d(g):
        for p in range(N):
            got("s", g, p)
        got("sa", g)
        ACC[...] = jnp.zeros_like(ACC)

        @pl.loop(0, 2 * N)
        def _(q):
            for j in range(2):
                piece = pl.ds(j * half, half)
                ACC[piece, :] += dot(XB[q, g, piece, :], WG[q, j, B, :]) + dot(XA[q, g, piece, :], WG[q, j, A, :])

        acc = ACC[...]
        HID[...] = (jax.nn.silu(acc[:, :ff]) * acc[:, ff:]).astype(BF16)

        def down_of(q):
            for j in range(2):
                piece = pl.ds(j * half, half)
                result = dot(HID[piece, :], WD[q, j]).astype(BF16)
                XA[q, g, piece, :] = result[:, :a_cols]
                XB[q, g, piece, :] = result[:, a_cols:]

        pl.loop(N, 2 * N)(down_of)
        start("S", g)
        start("SA", g)
        for k in ("r", "l", "rr", "ll", "sa"):
            sent(k, g)
        for p in range(N):
            sent("s", g, p)
        pl.loop(0, N)(down_of)

    def add(n, to, terms):
        @pl.loop(0, n // SUB)
        def _(i):
            at = pl.ds(pl.multiple_of(i * SUB, SUB), SUB)
            total = terms[0][at, :].astype(F32)
            for t in terms[1:]:
                total = total + t[at, :].astype(F32)
            to[at, :] = total.astype(BF16)

    def sum_at(p, g, *more):
        add(rows, XB.at[p, g], [XB.at[p, g], SB.at[p, g], *more])

    def sum_part(p, g, part, *more):
        add(half, XB.at[p, g, part], [XB.at[p, g, part], SB.at[p, g, part], *more])

    def release(g):
        sent("yt", g)
        sent("ta", g)
        pl.semaphore_signal(free.at[g - 1], inc=1, device_id=y_up[g], device_id_type=MESH)

    def stage_e(g):
        got("S", g)
        sum_at(3, g)
        start("or", g)
        start("ol", g)
        sum_part(2, g, hi)
        start("ir", g, 0)
        sum_part(1, g, lo)
        start("il", g, 0)
        got("SA", g)
        for p in range(N):
            add(rows, XA.at[p, g], [XA.at[p, g], SA.at[p, g]])
        if g:
            pl.semaphore_wait(free.at[g - 1], 1)
            start("ya", g)

    def stage_f(g):
        got("or", g)
        sum_part(2, g, lo, OP.at[0, g])
        start("ir", g, 1)
        got("ol", g)
        sum_part(1, g, hi, OP.at[1, g])
        start("il", g, 1)

    def stage_g(g):
        for k in range(2):
            got("ir", g, k)
            got("il", g, k)
        sum_at(0, g, IN.at[0, g], IN.at[1, g])
        if g:
            start("yo", g)

    def combine(g, first, parts):
        @pl.loop(0, N)
        def _(d):
            at = pl.ds(pl.multiple_of(d * tok, tok), tok)
            for j in range(2):
                i = 2 * g + j
                slots = lax.broadcasted_iota(jnp.int32, (half, tok), 0).astype(F32)
                takes = jnp.where(slots == SLOT[i : i + 1, at], GATE[i : i + 1, at], 0.0).astype(BF16)
                for from_, total in parts:
                    product = lax.dot_general(
                        takes, from_[j * half : (j + 1) * half, :], (((0,), (0,)), ((), ())), preferred_element_type=F32
                    )
                    total[at, :] = product if first and j == 0 else total[at, :] + product

    def stage_h(g, first=False):
        if g:
            got("yo", g)
        combine(g, first, [(PL.at[g - 1] if g else XB.at[0, 0], CB)])

    def stage_ha(g, first=False):
        if g:
            got("ya", g)
        combine(g, first, [(PA.at[g - 1, p] if g else XA.at[p, 0], CA.at[p]) for p in range(N)])

    weights(5, 10)
    stage_b(0)
    stage_a(1)
    stage_a(3)
    for d in range(1, N):
        got("za", d)
    for g in (1, 3, 2):
        place(g, [(TA.at[:, p], PA.at[g - 1, p]) for p in range(N)])
        start("ta", g)
    place(0, [(TA.at[:, p], XA.at[p, 0]) for p in range(N)])
    stage_c(0)
    weights(10, 13)
    stage_b(1)
    stage_a(2)
    weights(13, 16)
    for load in loads:
        load.wait()
    stage_d(0)
    stage_b(3)
    stage_c(1)
    stage_d(1)
    for g in (1, 3, 2):
        release(g)
    stage_c(3)
    stage_b(2)
    stage_e(1)
    stage_d(3)
    stage_f(1)
    stage_c(2)
    stage_e(3)
    stage_d(2)
    stage_g(1)
    stage_f(3)
    stage_e(2)
    stage_g(3)
    stage_f(2)
    stage_ha(1, True)
    stage_ha(3)
    stage_e(0)
    stage_ha(2)
    stage_ha(0)
    for d in range(1, N):
        sent("za", d)
    for d in (1, 3, 2):
        TA[d] = CA[:, d * tok : (d + 1) * tok, :].astype(BF16)
        start("zoa", d)
    stage_h(1, True)
    stage_f(0)
    stage_g(2)
    stage_h(3)
    stage_h(2)
    stage_g(0)
    stage_h(0)
    for d in (1, 3, 2):
        T[d] = CB[d * tok : (d + 1) * tok, :].astype(BF16)
        start("zo", d)
    total = CA[:, 0:tok, :]
    for d in range(1, N):
        got("zoa", d)
        total = total + ZA[d - 1].astype(F32)
    CA[0, 0:tok, :] = total[0]
    TA[0] = total.astype(BF16)
    for p in range(1, N):
        start("xo", p)
    total = CB[0:tok, :]
    for d in range(1, N):
        got("zo", d)
        total = total + ZR[d - 1].astype(F32)
    out[:, B] = total.astype(BF16)
    total = CA[0, 0:tok, :]
    for p in range(1, N):
        got("xo", p)
        total = total + XR[back[p] - 1].astype(F32)
    out[:, A] = total.astype(BF16)
    for key in copies:
        sent(*key)


def on_device(tokens, expert_ids, gate_weights, gate_up, down_proj):
    tok, width = tokens.shape
    top = expert_ids.shape[1]
    exp_dev, deep, _, ff = gate_up.shape
    cap = 9 * tok * top // (8 * exp_dev * N * N)
    half = N * cap
    rows = exp_dev * half
    a_cols = 256
    b_cols = width - a_cols
    flops = 2 * N * rows * deep * ff * 3
    n_copies = 11 * (N - 1) + 17 * N
    return pl.pallas_call(
        lambda *refs: kernel(cap, a_cols, *refs),
        out_shape=jax.ShapeDtypeStruct((tok, width), BF16),
        in_specs=[pl.BlockSpec(memory_space=pltpu.VMEM)] * 3 + [pl.BlockSpec(memory_space=pl.ANY)] * 2,
        out_specs=pl.BlockSpec(memory_space=pltpu.VMEM),
        scratch_shapes=[
            pltpu.VMEM((2 * N, N, rows, a_cols), BF16),
            pltpu.VMEM((2 * N, N, rows, b_cols), BF16),
            pltpu.VMEM((N, N, rows, a_cols), BF16),
            pltpu.VMEM((N, N, rows, b_cols), BF16),
            pltpu.VMEM((2, N, half, b_cols), BF16),
            pltpu.VMEM((2, N, rows, b_cols), BF16),
            pltpu.VMEM((N - 1, rows, b_cols), BF16),
            pltpu.VMEM((N - 1, N, rows, a_cols), BF16),
            pltpu.VMEM((N, tok, b_cols), BF16),
            pltpu.VMEM((N, N, tok, a_cols), BF16),
            pltpu.VMEM((N, 2 * top, tok), F32),
            pltpu.VMEM((N - 1, tok, b_cols), BF16),
            pltpu.VMEM((N - 1, N, tok, a_cols), BF16),
            pltpu.VMEM((N - 1, tok, a_cols), BF16),
            pltpu.VMEM((N * tok, b_cols), F32),
            pltpu.VMEM((N, N * tok, a_cols), F32),
            pltpu.VMEM((rows, 2 * ff), F32),
            pltpu.VMEM((rows, ff), BF16),
            pltpu.VMEM((2 * N, N * tok), F32),
            pltpu.VMEM((2 * N, N * tok), F32),
            pltpu.VMEM((2 * N, exp_dev, width, 2 * ff), BF16),
            pltpu.VMEM((2 * N, exp_dev, ff, width), BF16),
            pltpu.VMEM((2, width, 2, ff), BF16),
            pltpu.SemaphoreType.REGULAR((N - 1,)),
            pltpu.SemaphoreType.DMA((2 * N,)),
            pltpu.SemaphoreType.DMA((2,)),
            pltpu.SemaphoreType.DMA((n_copies,)),
            pltpu.SemaphoreType.DMA((n_copies,)),
        ],
        compiler_params=pltpu.CompilerParams(
            collective_id=0, has_side_effects=True, vmem_limit_bytes=62 << 20
        ),
        cost_estimate=pl.CostEstimate(flops=flops, bytes_accessed=24 << 20, transcendentals=0),
    )(tokens, expert_ids.T, gate_weights.T, gate_up, down_proj)


def solution(mesh):
    placed = (
        P("expert", "etensor"),
        P("expert", None),
        P("expert", None),
        P("expert", None, None, "etensor"),
        P("expert", "etensor", None),
    )
    return jax.shard_map(
        on_device, mesh=mesh, in_specs=placed, out_specs=P("expert", "etensor"), check_vma=False
    )
```
